32 devices in a mesh: sector: 4 (over y, core), owner: 8 (over z, x).
Axes of the slice: x: 2, y: 2, z: 4, core: 2. Of those that a mesh axis runs over, the one named last changes fastest.
Arguments:
- broadcast_ops: float32 [4, 4, 1024, 1024], P('sector', None, 'owner'), may hold values from -0.1875 to 0.1875
- resident_ops: float32 [4, 8, 1024, 1024], P('sector', 'owner'), may hold values from -6 to 6
- integrals: float32 [4, 8, 4, 4], P('sector', 'owner'), may hold values from -3 to 3
- owner_list: int32 [8, 4], P('owner'), may hold values from 0 to 3, as said below
Outputs:
- complementary: float32 [4, 8, 2, 1024, 1024], P('sector', 'owner')
The draws below stay inside these ranges and needn't reach their ends.
Inputs may be any that keep to these rules, and one draw needn't show every extreme that they name: `owner_list`: in each row one sector group is named exactly 2 times, one is not named, and every other is named once.
All inputs are finite; a program needn't handle non-finite values.
Results may differ from the reference program's by a relative error of at most 0.012.
Values may be sent and summed in bfloat16 or wider, within the bound.
No kernel may reach another device: no remote copies, remote signals or barrier semaphores. Data moves between devices by JAX's collectives and lax.ppermute only.
A program may use at most 64 MiB of HBM per device.

```python
import jax
import jax.numpy as jnp
from jax import lax

M = 1024
NB = 4
CAP = 2
PAIRS = 4
N_SECTOR = 4
N_OWNER = 8


def draw_owner_list(key, part):
    row_keys = jax.random.split(key, N_OWNER)

    def draw_row(row_key):
        first_key, second_key = jax.random.split(row_key)
        sector_order = jax.random.permutation(first_key, N_SECTOR).astype(jnp.int32)
        row_sectors = sector_order.at[N_SECTOR - 1].set(sector_order[0])
        return jax.random.permutation(second_key, row_sectors).astype(jnp.int32)
    return jax.vmap(draw_row)(row_keys)


def block_levels(rng, dims, cuts, least, high):
    level, own = 1.0, jax.random.fold_in(rng, 6)
    for position, blocks in cuts:
        steps = jnp.exp(jax.random.uniform(jax.random.fold_in(own, position), (blocks,), jnp.float32, least / len(cuts), high / len(cuts)))
        level = level * jnp.repeat(steps, dims[position] // blocks).reshape([-1 if axis == position else 1 for axis in range(len(dims))])
    return level


def centred(stream_key, extent, width, bound, shards=(), held_as=jnp.bfloat16):
    gain = block_levels(stream_key, extent, shards, -0.22, 0.18) if shards else 1.0
    entries = jax.random.normal(stream_key, extent, jnp.float32) * width * gain
    return jnp.minimum(jnp.maximum(entries, -bound), bound).astype(held_as)


def setup_inputs(seed: int = 0) -> dict:
    arg_keys = jax.random.split(jax.random.key(seed), 5)
    return {
        "broadcast_ops": centred(arg_keys[0], (N_SECTOR, NB, M, M), M ** -0.5, 0.1875, ((0, 4), (2, 8)), jnp.float32),
        "resident_ops": centred(arg_keys[1], (N_SECTOR, N_OWNER, M, M), 1.0, 6.0, ((0, 4), (1, 8)), jnp.float32),
        "integrals": centred(arg_keys[2], (N_SECTOR, N_OWNER, PAIRS, NB), 0.5, 3.0, ((0, 4), (1, 8)), jnp.float32),
        "owner_list": draw_owner_list(jax.random.fold_in(arg_keys[4], 71), 0),
    }


def reference(broadcast_ops, resident_ops, integrals, owner_list):
    highest = lax.Precision.HIGHEST

    def owner_part(pair):
        resident, weights = pair
        return resident, weights

    pair_total = jnp.zeros((N_OWNER, PAIRS, M, M), jnp.float32)
    for sector_id in range(N_SECTOR):
        shared = broadcast_ops[sector_id]

        def one_owner(pair):
            resident, weights = pair
            products = jnp.einsum("kmj,jn->kmn", shared, resident, precision=highest)
            return jnp.einsum("pk,kmn->pmn", weights, products, precision=highest)

        partial_ops = lax.map(one_owner, (resident_ops[sector_id], integrals[sector_id]))
        rounded = lax.optimization_barrier(partial_ops.astype(jnp.bfloat16))
        pair_total = pair_total + rounded.astype(jnp.float32)
    same_owner = owner_list[:, :, None] == owner_list[:, None, :]
    earlier = jnp.arange(PAIRS)[None, :, None] < jnp.arange(PAIRS)[None, None, :]
    slot_rank = jnp.sum((same_owner & earlier).astype(jnp.int32), axis=1)
    sectors = jnp.arange(N_SECTOR)[:, None, None, None]
    slots = jnp.arange(CAP)[None, None, :, None]
    selector = ((owner_list[None, :, None, :] == sectors) & (slot_rank[None, :, None, :] == slots)).astype(jnp.float32)
    return jnp.einsum("docp,opmn->docmn", selector, pair_total, precision=highest)
```

```python
import functools

import jax
import jax.numpy as jnp
from jax import lax
from jax.experimental import pallas as pl
from jax.experimental.pallas import tpu as pltpu
from jax.sharding import PartitionSpec as P

CAP = 2
BF16 = jnp.bfloat16
F32 = jnp.float32


def ring_order(n):
    return list(range(0, n, 2)) + list(range(1, n, 2))[::-1]


def plan_of(owners_ref, side):
    n = owners_ref.shape[1]
    own = [owners_ref[0, p] for p in range(n)]
    rank, key = [], []
    for p in range(n):
        r = jnp.int32(0)
        for q in range(p):
            r = r + (own[q] == own[p]).astype(jnp.int32)
        rank.append(r)
        key.append(own[p] * CAP + r)
    place = []
    for p in range(n):
        r = jnp.int32(0)
        for q in range(n):
            if q != p:
                r = r + (key[q] < key[p]).astype(jnp.int32)
        place.append(jnp.where(side == 0, r, n - 1 - r))
    pair_at = []
    for i in range(n):
        r = jnp.int32(0)
        for p in range(n):
            r = r + jnp.where(place[p] == i, p, 0)
        pair_at.append(r)

    def slot_place(sector, slot):
        r = jnp.int32(-1)
        for p in range(n):
            r = jnp.where((own[p] == sector) & (rank[p] == slot), place[p], r)
        return r

    return pair_at, slot_place


def step_kernel(cfg, *refs):
    names = cfg["names"]
    r = dict(zip(names, refs, strict=True))
    lanes, half, n_owner = cfg["lanes"], cfg["half"], cfg["n_owner"]
    pairs, sent = cfg["pairs"], cfg["sent"]
    ids = r["ids"]
    side, core, q = ids[0], ids[1], ids[2]
    pair_at, slot_place = plan_of(r["owners"], side)
    sector = side * 2 + core
    other = side * 2 + 1 - core
    m, depth = cfg["m"], cfg["m"]
    if cfg["compute"] is not None:
        loads = []
        for t in range(cfg["tiles"]):
            w = m // cfg["tiles"]
            for s, name in enumerate(("res0", "res1")):
                c = pltpu.make_async_copy(
                    r[name].at[:, pl.ds(t * w, w)],
                    r["rbuf"].at[t, pl.ds(s * depth, depth), :],
                    r["rsem"].at[t, s],
                )
                c.start()
                loads.append(c)

    def rows_of(step, lane, which):
        turn, start, _ = lanes[lane]
        at = lax.rem(q - turn * step + 2 * n_owner, n_owner)
        owner = jnp.where(at < n_owner // 2, 2 * at, 2 * (n_owner - 1 - at) + 1)
        return pl.multiple_of(owner * (2 * half) + which * half + start, 8)

    stores = []

    def store(buf, step, which, sem):
        for lane, (_, start, rows) in enumerate(lanes):
            c = pltpu.make_async_copy(
                r[buf].at[:, pl.ds(start, rows), :],
                r["out"].at[:, pl.ds(rows_of(step, lane, which), rows), :],
                r["osem"].at[sem, lane],
            )
            c.start()
            stores.append(c)

    if cfg["finish"] is not None:
        for slot in range(CAP):
            place = slot_place(other, slot)
            i = jnp.maximum(place, 0)
            v = r["kept_in"][i] + r["crossed"][sent - 1 - i].astype(F32)
            r["swap_out"][slot] = v.astype(BF16)
        for slot in range(CAP):
            place = slot_place(sector, slot)
            i = jnp.maximum(place, 0)
            v = r["kept_in"][i] + r["crossed"][sent - 1 - i].astype(F32)
            r["fin"][slot] = jnp.where(place >= 0, v, 0.0)
        store("fin", cfg["finish"], core, 0)
    if cfg["place"] is not None:
        for slot in range(CAP):
            place = slot_place(sector, slot)
            r["fin2"][slot] = jnp.where(place >= 0, r["swapped"][slot].astype(F32), 0.0)
        store("fin2", cfg["place"], 1 - core, 1)

    if cfg["compute"] is not None:
        nb = cfg["nb"]
        for s, wname in enumerate(("w0", "w1")):
            for lane, (_, start, rows) in enumerate(lanes):
                x = [r[f"x{lane}"][s, k].astype(F32) for k in range(nb)]
                for i in range(pairs):
                    a = r[wname][pair_at[i], 0] * x[0]
                    for k in range(1, nb):
                        a = a + r[wname][pair_at[i], k] * x[k]
                    r["abuf"][pl.ds(i * half + start, rows), pl.ds(s * depth, depth)] = a.astype(BF16)
        w = m // cfg["tiles"]
        for t in range(cfg["tiles"]):
            loads[2 * t].wait()
            loads[2 * t + 1].wait()
            y = jnp.dot(r["abuf"][...], r["rbuf"][t], preferred_element_type=F32)
            y = y.reshape(pairs, half, w)
            r["send"][:, :, pl.ds(t * w, w)] = y[pairs - sent :].astype(BF16)
            r["kept"][:, :, pl.ds(t * w, w)] = y[:sent]
    for c in stores:
        c.wait()


def step_call(static, compute, finish, place, common, xs, res, kept, crossed, swapped, out):
    m, half, lanes, pairs, sent = (static[k] for k in ("m", "half", "lanes", "pairs", "sent"))
    smem = pl.BlockSpec(memory_space=pltpu.SMEM)
    vmem = pl.BlockSpec(memory_space=pltpu.VMEM)
    anym = pl.BlockSpec(memory_space=pl.ANY)
    names, args, specs = [], [], []

    def add(name, arg, spec):
        names.append(name)
        args.append(arg)
        specs.append(spec)

    for name in ("ids", "owners"):
        add(name, common[name], smem)
    if compute is not None:
        for name in ("w0", "w1"):
            add(name, common[name], smem)
        for lane, x in enumerate(xs):
            add(f"x{lane}", x, vmem)
        add("res0", res[0], anym)
        add("res1", res[1], anym)
    if finish is not None:
        add("kept_in", kept, vmem)
        add("crossed", crossed, vmem)
    if place is not None:
        add("swapped", swapped, vmem)
    aliases = {}
    writes = finish is not None or place is not None
    if writes and out is not None:
        aliases[len(names)] = "out"
        add("out_in", out, anym)
    outs, shapes, ospecs = [], [], []

    def give(name, shape, dtype, spec):
        outs.append(name)
        shapes.append(jax.ShapeDtypeStruct(shape, dtype))
        ospecs.append(spec)

    if compute is not None:
        give("send", (sent, half, m), BF16, vmem)
        give("kept", (sent, half, m), F32, vmem)
    if finish is not None:
        give("swap_out", (CAP, half, m), BF16, vmem)
    if writes:
        give("out", (CAP, m, m), F32, anym)
    aliases = {i: outs.index(n) for i, n in aliases.items()}
    scratch, snames = [], []

    def hold(name, s):
        snames.append(name)
        scratch.append(s)

    tiles = 4
    if compute is not None:
        hold("abuf", pltpu.VMEM((pairs * half, 2 * m), BF16))
        hold("rbuf", pltpu.VMEM((tiles, 2 * m, m // tiles), BF16))
        hold("rsem", pltpu.SemaphoreType.DMA((tiles, 2)))
    if finish is not None:
        hold("fin", pltpu.VMEM((CAP, half, m), F32))
    if place is not None:
        hold("fin2", pltpu.VMEM((CAP, half, m), F32))
    if writes:
        hold("osem", pltpu.SemaphoreType.DMA((2, len(lanes))))
    cfg = dict(static, compute=compute, finish=finish, place=place, tiles=tiles, names=names + outs + snames)
    flops = 2 * pairs * half * 2 * m * m if compute is not None else 2 * half * m
    got = pl.pallas_call(
        functools.partial(step_kernel, cfg),
        in_specs=specs,
        out_specs=ospecs,
        out_shape=shapes,
        scratch_shapes=scratch,
        input_output_aliases=aliases,
        compiler_params=pltpu.CompilerParams(vmem_limit_bytes=32 * 1024 * 1024),
        cost_estimate=pl.CostEstimate(flops=flops, bytes_accessed=8 * m * m, transcendentals=0),
    )(*args)
    return dict(zip(outs, got, strict=True))


def shards(broadcast_ops, resident_ops, integrals, owner_list):
    n_sector = lax.axis_size("sector")
    n_owner = lax.axis_size("owner")
    sector = lax.axis_index("sector")
    owner = lax.axis_index("owner")
    nb, rows, m = broadcast_ops.shape[1:]
    pairs = owner_list.shape[1]
    half = rows // 2
    core = sector % 2
    swap_core = [(i, i ^ 1) for i in range(n_sector)]
    swap_side = [(i, (i + 2) % n_sector) for i in range(n_sector)]
    order = ring_order(n_owner)
    up = [(order[i], order[(i + 1) % n_owner]) for i in range(n_owner)]
    down = [(b, a) for a, b in up]
    if half % 32 == 0:
        lanes = ((1, 0, half // 2), (-1, half // 2, half // 2))
    else:
        lanes = ((1, 0, half),)
    static = dict(m=m, nb=nb, half=half, lanes=lanes, n_owner=n_owner, pairs=pairs, sent=min(pairs, CAP + 1))

    shared = broadcast_ops[0]
    theirs = lax.dynamic_slice_in_dim(shared, (1 - core) * half, half, 1).astype(BF16)
    mine = lax.dynamic_slice_in_dim(shared, core * half, half, 1).astype(BF16)
    arrived = lax.ppermute(theirs, "sector", swap_core)
    res_own = resident_ops[0, 0].astype(BF16)
    w_own = integrals[0, 0]
    w_other = lax.ppermute(w_own, "sector", swap_core)
    res_other = lax.ppermute(res_own, "sector", swap_core)
    xs = [jnp.stack([mine[:, a : a + n], arrived[:, a : a + n]]) for _, a, n in lanes]
    q = jnp.where(owner % 2 == 0, owner // 2, n_owner - 1 - owner // 2)
    common = {
        "ids": jnp.stack([sector // 2, core, q]).astype(jnp.int32),
        "owners": owner_list,
        "w0": w_own,
        "w1": w_other,
    }
    res = (res_own, res_other)
    out, kept, crossed, swapped = None, None, None, None
    for step in range(n_owner + 2):
        compute = step if step < n_owner else None
        finish = step - 1 if 1 <= step <= n_owner else None
        place = step - 2 if step >= 2 else None
        later = xs
        if step < n_owner - 1:
            later = [
                lax.ppermute(x, "owner", up if turn == 1 else down) for x, (turn, _, _) in zip(xs, lanes, strict=True)
            ]
        got = step_call(static, compute, finish, place, common, xs, res, kept, crossed, swapped, out)
        if compute is not None:
            kept, crossed = got["kept"], lax.ppermute(got["send"], "sector", swap_side)
        if finish is not None:
            swapped = lax.ppermute(got["swap_out"], "sector", swap_core)
        if "out" in got:
            out = got["out"]
        xs = later
    return out[None, None]


def solution(mesh):
    in_specs = (
        P("sector", None, "owner", None),
        P("sector", "owner", None, None),
        P("sector", "owner", None, None),
        P("owner", None),
    )
    out_specs = P("sector", "owner", None, None, None)
    return jax.shard_map(shards, mesh=mesh, in_specs=in_specs, out_specs=out_specs, check_vma=False)
```

```python
import functools

import jax
import jax.numpy as jnp
from jax import lax
from jax.experimental import pallas as pl
from jax.experimental.pallas import tpu as pltpu
from jax.sharding import PartitionSpec as P

CAP = 2
KERNEL_COST = 4 * 10**9
FINISH_LAG = 1
PLACE_LAG = 0
LANES = 128
BF16 = jnp.bfloat16
F32 = jnp.float32


def ring_order(n):
    return list(range(0, n, 2)) + list(range(1, n, 2))[::-1]


def plan_of(owners_ref, side):
    n = owners_ref.shape[1]
    own = [owners_ref[0, p] for p in range(n)]
    rank, key = [], []
    for p in range(n):
        r = jnp.int32(0)
        for q in range(p):
            r = r + (own[q] == own[p]).astype(jnp.int32)
        rank.append(r)
        key.append(own[p] * CAP + r)
    place = []
    for p in range(n):
        r = jnp.int32(0)
        for q in range(n):
            if q != p:
                r = r + (key[q] < key[p]).astype(jnp.int32)
        place.append(jnp.where(side == 0, r, n - 1 - r))
    pair_at = []
    for i in range(n):
        r = jnp.int32(0)
        for p in range(n):
            r = r + jnp.where(place[p] == i, p, 0)
        pair_at.append(r)

    def slot_place(sector, slot):
        r = jnp.int32(-1)
        for p in range(n):
            r = jnp.where((own[p] == sector) & (rank[p] == slot), place[p], r)
        return r

    return pair_at, slot_place


def prepare(r, m):
    ids, meta, spread = r["ids"], r["meta"], r["spread"]
    side, core = ids[0], ids[1]
    pair_at, slot_place = plan_of(r["owners"], side)
    for slot in range(CAP):
        meta[0, slot] = slot_place(side * 2 + core, slot)
        meta[0, CAP + slot] = slot_place(side * 2 + 1 - core, slot)
    meta[0, 2 * CAP] = core
    meta[0, 2 * CAP + 1] = ids[2]
    for s in range(2):
        w = r[f"w{s}"]
        nb = w.shape[1]
        for i, pair in enumerate(pair_at):
            for k in range(nb):
                row = (s * len(pair_at) + i) * nb + k
                spread[pl.ds(row, 1), :] = jnp.full((1, LANES), w[pair, k], F32)
        r["res"][pl.ds(s * m, m), :] = r[f"res{s}"][...]


def step_kernel(cfg, *refs):
    r = dict(zip(cfg["names"], refs, strict=True))
    half, n_owner, m, nb = cfg["half"], cfg["n_owner"], cfg["m"], cfg["nb"]
    pairs, sent = cfg["pairs"], cfg["sent"]
    if cfg["first"]:
        prepare(r, m)
    place_of = [r["meta"][0, slot] for slot in range(CAP)]
    other_of = [r["meta"][0, CAP + slot] for slot in range(CAP)]
    core, q = r["meta"][0, 2 * CAP], r["meta"][0, 2 * CAP + 1]
    stores = []

    def store(buf, sem, unit, which):
        base = 0
        for lane, (step, turn, start, rows) in enumerate(unit):
            at = lax.rem(q - turn * step + 2 * n_owner, n_owner)
            owner = jnp.where(at < n_owner // 2, 2 * at, 2 * (n_owner - 1 - at) + 1)
            row = pl.multiple_of(owner * (2 * half) + which * half + start, 8)
            c = pltpu.make_async_copy(
                r[buf].at[:, pl.ds(base, rows), :], r["out"].at[:, pl.ds(row, rows), :], r[sem].at[lane]
            )
            c.start()
            stores.append(c)
            base += rows

    for j, unit in enumerate(cfg["finish"]):
        kept, crossed, fin = r[f"kept{j}"], r[f"crossed{j}"], r[f"fin{j}"]
        for slot in range(CAP):
            i = jnp.maximum(other_of[slot], 0)
            r[f"swap{j}"][slot] = (kept[i] + crossed[sent - 1 - i].astype(F32)).astype(BF16)
        for slot in range(CAP):
            place = place_of[slot]
            i = jnp.maximum(place, 0)
            fin[slot] = jnp.where(place >= 0, kept[i] + crossed[sent - 1 - i].astype(F32), 0.0)
        store(f"fin{j}", f"finsem{j}", unit, core)
    for j, unit in enumerate(cfg["place"]):
        for slot in range(CAP):
            v = r[f"swapped{j}"][slot].astype(F32)
            r[f"put{j}"][slot] = jnp.where(place_of[slot] >= 0, v, 0.0)
        store(f"put{j}", f"putsem{j}", unit, 1 - core)

    if cfg["compute"] is not None:
        unit = cfg["compute"]
        total = sum(block[-1] for block in unit)
        for s in range(2):
            base = 0
            for lane, (*_, rows) in enumerate(unit):
                for c in range(0, m, LANES):
                    cols = pl.ds(c, LANES)
                    x = [r[f"x{lane}"][s, k, :, cols].astype(F32) for k in range(nb)]
                    for i in range(pairs):
                        row = (s * pairs + i) * nb
                        a = r["spread"][pl.ds(row, 1), :] * x[0]
                        for k in range(1, nb):
                            a = a + r["spread"][pl.ds(row + k, 1), :] * x[k]
                        r["abuf"][pl.ds(i * total + base, rows), pl.ds(s * m + c, LANES)] = a.astype(BF16)
                base += rows
        w = m // cfg["tiles"]
        for t in range(cfg["tiles"]):
            cols = pl.ds(t * w, w)
            y = jnp.dot(r["abuf"][...], r["res"][:, cols], preferred_element_type=F32)
            y = y.reshape(pairs, total, w)
            r["send"][:, :, cols] = y[pairs - sent :].astype(BF16)
            r["kept"][:, :, cols] = y[:sent]
    r["token"][...] = jnp.zeros_like(r["token"])
    for c in stores:
        c.wait()


def step_call(static, common, out, compute=None, finish=(), place=(), after=()):
    m, pairs, sent = static["m"], static["pairs"], static["sent"]
    smem = pl.BlockSpec(memory_space=pltpu.SMEM)
    vmem = pl.BlockSpec(memory_space=pltpu.VMEM)
    anym = pl.BlockSpec(memory_space=pl.ANY)
    names, args, specs = [], [], []
    outs, shapes, ospecs = [], [], []
    snames, scratch = [], []

    def take(name, arg, spec):
        names.append(name)
        args.append(arg)
        specs.append(spec)

    def give(name, shape, dtype, spec):
        outs.append(name)
        shapes.append(jax.ShapeDtypeStruct(shape, dtype))
        ospecs.append(spec)

    def hold(name, what):
        snames.append(name)
        scratch.append(what)

    def rows_in(unit):
        return sum(block[-1] for block in unit)

    first = "meta" not in common
    if first:
        for name in ("ids", "owners", "w0", "w1"):
            take(name, common[name], smem)
        for name in ("res0", "res1"):
            take(name, common[name], vmem)
        give("meta", (1, 2 * CAP + 2), jnp.int32, smem)
        give("spread", (2 * pairs * static["nb"], LANES), F32, vmem)
        give("res", (2 * m, m), BF16, vmem)
    else:
        take("meta", common["meta"], smem)
    flops = 0
    if compute is not None:
        unit, xs = compute
        total = rows_in(unit)
        if not first:
            take("res", common["res"], vmem)
        if not first:
            take("spread", common["spread"], vmem)
        for lane, x in enumerate(xs):
            take(f"x{lane}", x, vmem)
        give("send", (sent, total, m), BF16, vmem)
        give("kept", (sent, total, m), F32, vmem)
        hold("abuf", pltpu.VMEM((pairs * total, 2 * m), BF16))
        flops += 2 * pairs * total * 2 * m * m
    for j, (unit, kept, crossed) in enumerate(finish):
        take(f"kept{j}", kept, vmem)
        take(f"crossed{j}", crossed, vmem)
        give(f"swap{j}", (CAP, rows_in(unit), m), BF16, vmem)
        hold(f"fin{j}", pltpu.VMEM((CAP, rows_in(unit), m), F32))
        hold(f"finsem{j}", pltpu.SemaphoreType.DMA((len(unit),)))
    for j, (unit, swapped) in enumerate(place):
        take(f"swapped{j}", swapped, vmem)
        hold(f"put{j}", pltpu.VMEM((CAP, rows_in(unit), m), F32))
        hold(f"putsem{j}", pltpu.SemaphoreType.DMA((len(unit),)))
    for j, x in enumerate(after):
        take(f"after{j}", x, anym)
    give("token", (8, LANES), F32, vmem)
    aliases = {}
    if finish or place:
        give("out", (CAP, m, m), F32, anym)
        if out is not None:
            aliases[len(names)] = outs.index("out")
            take("out_in", out, anym)
    cfg = dict(
        static,
        first=first,
        compute=None if compute is None else compute[0],
        finish=[f[0] for f in finish],
        place=[p[0] for p in place],
        tiles=4,
        names=names + outs + snames,
    )
    got = pl.pallas_call(
        functools.partial(step_kernel, cfg),
        in_specs=specs,
        out_specs=ospecs,
        out_shape=shapes,
        scratch_shapes=scratch,
        input_output_aliases=aliases,
        compiler_params=pltpu.CompilerParams(vmem_limit_bytes=24 * 1024 * 1024),
        cost_estimate=pl.CostEstimate(flops=KERNEL_COST, bytes_accessed=1000, transcendentals=0),
    )(*args)
    return dict(zip(outs, got, strict=True))


def shards(broadcast_ops, resident_ops, integrals, owner_list):
    n_sector = lax.axis_size("sector")
    n_owner = lax.axis_size("owner")
    sector = lax.axis_index("sector")
    owner = lax.axis_index("owner")
    nb, rows, m = broadcast_ops.shape[1:]
    pairs = owner_list.shape[1]
    half = rows // 2
    core = sector % 2
    swap_core = [(i, i ^ 1) for i in range(n_sector)]
    swap_side = [(i, (i + 2) % n_sector) for i in range(n_sector)]
    order = ring_order(n_owner)
    up = [(order[i], order[(i + 1) % n_owner]) for i in range(n_owner)]
    down = [(b, a) for a, b in up]
    if half % 32 == 0:
        lanes = [(1, 0, half // 2), (-1, half // 2, half // 2)]
    else:
        lanes = [(1, 0, half)]
    cuts = 2 if lanes[0][2] % 32 == 0 else 1
    static = dict(m=m, nb=nb, half=half, n_owner=n_owner, pairs=pairs, sent=min(pairs, CAP + 1))

    shared = broadcast_ops[0]
    theirs = lax.dynamic_slice_in_dim(shared, (1 - core) * half, half, 1).astype(BF16)
    arrived = lax.ppermute(theirs, "sector", swap_core)
    mine = lax.dynamic_slice_in_dim(shared, core * half, half, 1).astype(BF16)
    xs = [jnp.stack([mine[:, a : a + n], arrived[:, a : a + n]]) for _, a, n in lanes]
    resident, *xs = lax.optimization_barrier((resident_ops[0, 0], *xs))
    res_own = resident.astype(BF16)
    w_own = integrals[0, 0]
    w_other = lax.ppermute(w_own, "sector", swap_core)
    res_other = lax.ppermute(res_own, "sector", swap_core)
    q = jnp.where(owner % 2 == 0, owner // 2, n_owner - 1 - owner // 2)
    ids = jnp.stack([sector // 2, core, q]).astype(jnp.int32)
    common = {"ids": ids, "owners": owner_list, "w0": w_own, "w1": w_other, "res0": res_own, "res1": res_other}

    def send_on(x, turn):
        return lax.ppermute(x, "owner", up if turn == 1 else down)

    units, kept, crossed, swapped = [], {}, {}, {}
    to_finish, to_place = [], []
    state = {"out": None, "token": None}

    def call(unit, rows, n_finish, n_place):
        finish = [to_finish.pop(0) for _ in range(max(0, n_finish))]
        place = [to_place.pop(0) for _ in range(max(0, n_place))]
        got = step_call(
            static,
            common,
            state["out"],
            None if unit is None else (unit, rows),
            [(units[f], kept[f], crossed[f]) for f in finish],
            [(units[p], swapped[p]) for p in place],
            [] if state["token"] is None else [state["token"]],
        )
        common.update({name: got[name] for name in ("meta", "spread", "res") if name in got})
        state["out"], state["token"] = got.get("out", state["out"]), got["token"]
        if unit is not None:
            i = len(units)
            units.append(unit)
            kept[i] = got["kept"]
            crossed[i] = lax.ppermute(got["send"], "sector", swap_side)
            to_finish.append(i)
        for j, f in enumerate(finish):
            swapped[f] = lax.ppermute(got[f"swap{j}"], "sector", swap_core)
            to_place.append(f)

    last = n_owner - 1
    for step in range(last):
        unit = [(step, *lane) for lane in lanes]
        if state["token"] is not None:
            for i in range(len(xs) - 1, -1, -1):
                xs[i], state["token"] = lax.optimization_barrier((xs[i], state["token"]))
        if step < last - 1:
            then = [send_on(x, lane[0]) for x, lane in zip(xs, lanes, strict=True)]
        else:
            then = [[send_on(jnp.split(x, cuts, 2)[c], lane[0]) for x, lane in zip(xs, lanes, strict=True)] for c in range(cuts)]
        call(unit, xs, len(to_finish) - FINISH_LAG, len(to_place) - PLACE_LAG)
        xs = then
    for c in range(cuts):
        unit = [(last, turn, start + c * (rows // cuts), rows // cuts) for turn, start, rows in lanes]
        if c < cuts - 1:
            call(unit, xs[c], len(to_finish) - 1, len(to_place))
        else:
            call(unit, xs[c], 0, 0)
    call(None, None, len(to_finish), len(to_place))
    call(None, None, 0, len(to_place))
    return state["out"][None, None]


def solution(mesh):
    in_specs = (
        P("sector", None, "owner", None),
        P("sector", "owner", None, None),
        P("sector", "owner", None, None),
        P("owner", None),
    )
    out_specs = P("sector", "owner", None, None, None)
    return jax.shard_map(shards, mesh=mesh, in_specs=in_specs, out_specs=out_specs, check_vma=False)
```

```python
import functools

import jax
import jax.numpy as jnp
from jax import lax
from jax.experimental import pallas as pl
from jax.experimental.pallas import tpu as pltpu
from jax.sharding import PartitionSpec as P

CAP = 2
KERNEL_COST = 3 * 10**9
FINISH_LAG = 1
PLACE_LAG = 0
LANES = 128
BF16 = jnp.bfloat16
F32 = jnp.float32


def ring_order(n):
    return list(range(0, n, 2)) + list(range(1, n, 2))[::-1]


def plan_of(owners_ref, side):
    n = owners_ref.shape[1]
    own = [owners_ref[0, p] for p in range(n)]
    rank, key = [], []
    for p in range(n):
        r = jnp.int32(0)
        for q in range(p):
            r = r + (own[q] == own[p]).astype(jnp.int32)
        rank.append(r)
        key.append(own[p] * CAP + r)
    place = []
    for p in range(n):
        r = jnp.int32(0)
        for q in range(n):
            if q != p:
                r = r + (key[q] < key[p]).astype(jnp.int32)
        place.append(jnp.where(side == 0, r, n - 1 - r))
    pair_at = []
    for i in range(n):
        r = jnp.int32(0)
        for p in range(n):
            r = r + jnp.where(place[p] == i, p, 0)
        pair_at.append(r)

    def slot_place(sector, slot):
        r = jnp.int32(-1)
        for p in range(n):
            r = jnp.where((own[p] == sector) & (rank[p] == slot), place[p], r)
        return r

    return pair_at, slot_place


def prepare(r, m):
    ids, meta, spread = r["ids"], r["meta"], r["spread"]
    side, core = ids[0], ids[1]
    pair_at, slot_place = plan_of(r["owners"], side)
    for slot in range(CAP):
        meta[0, slot] = slot_place(side * 2 + core, slot)
        meta[0, CAP + slot] = slot_place(side * 2 + 1 - core, slot)
    meta[0, 2 * CAP] = core
    meta[0, 2 * CAP + 1] = ids[2]
    for s in range(2):
        w = r[f"w{s}"]
        nb = w.shape[1]
        for i, pair in enumerate(pair_at):
            for k in range(nb):
                row = (s * len(pair_at) + i) * nb + k
                spread[pl.ds(row, 1), :] = jnp.full((1, LANES), w[pair, k], F32)
        r["res"][pl.ds(s * m, m), :] = r[f"res{s}"][...]


def step_kernel(cfg, *refs):
    r = dict(zip(cfg["names"], refs, strict=True))
    half, n_owner, m, nb = cfg["half"], cfg["n_owner"], cfg["m"], cfg["nb"]
    pairs, sent = cfg["pairs"], cfg["sent"]
    if cfg["first"]:
        prepare(r, m)
    place_of = [r["meta"][0, slot] for slot in range(CAP)]
    other_of = [r["meta"][0, CAP + slot] for slot in range(CAP)]
    core, q = r["meta"][0, 2 * CAP], r["meta"][0, 2 * CAP + 1]
    stores = []

    def store(buf, sem, unit, which):
        base = 0
        for lane, (step, turn, start, rows) in enumerate(unit):
            at = lax.rem(q - turn * step + 2 * n_owner, n_owner)
            owner = jnp.where(at < n_owner // 2, 2 * at, 2 * (n_owner - 1 - at) + 1)
            row = pl.multiple_of(owner * (2 * half) + which * half + start, 8)
            c = pltpu.make_async_copy(
                r[buf].at[:, pl.ds(base, rows), :], r["out"].at[:, pl.ds(row, rows), :], r[sem].at[lane]
            )
            c.start()
            stores.append(c)
            base += rows

    for j, unit in enumerate(cfg["finish"]):
        kept, crossed, fin = r[f"kept{j}"], r[f"crossed{j}"], r[f"fin{j}"]
        for slot in range(CAP):
            i = jnp.maximum(other_of[slot], 0)
            r[f"swap{j}"][slot] = (kept[i] + crossed[sent - 1 - i].astype(F32)).astype(BF16)
        for slot in range(CAP):
            place = place_of[slot]
            i = jnp.maximum(place, 0)
            fin[slot] = jnp.where(place >= 0, kept[i] + crossed[sent - 1 - i].astype(F32), 0.0)
        store(f"fin{j}", f"finsem{j}", unit, core)
    for j, unit in enumerate(cfg["place"]):
        for slot in range(CAP):
            v = r[f"swapped{j}"][slot].astype(F32)
            r[f"put{j}"][slot] = jnp.where(place_of[slot] >= 0, v, 0.0)
        store(f"put{j}", f"putsem{j}", unit, 1 - core)

    if cfg["compute"] is not None:
        unit = cfg["compute"]
        total = sum(block[-1] for block in unit)
        for s in range(2):
            base = 0
            for lane, (*_, rows) in enumerate(unit):
                for c in range(0, m, LANES):
                    cols = pl.ds(c, LANES)
                    x = [r[f"x{lane}"][s, k, :, cols].astype(F32) for k in range(nb)]
                    for i in range(pairs):
                        row = (s * pairs + i) * nb
                        a = r["spread"][pl.ds(row, 1), :] * x[0]
                        for k in range(1, nb):
                            a = a + r["spread"][pl.ds(row + k, 1), :] * x[k]
                        r["abuf"][pl.ds(i * total + base, rows), pl.ds(s * m + c, LANES)] = a.astype(BF16)
                base += rows
        w = m // cfg["tiles"]
        for t in range(cfg["tiles"]):
            cols = pl.ds(t * w, w)
            y = jnp.dot(r["abuf"][...], r["res"][:, cols], preferred_element_type=F32)
            y = y.reshape(pairs, total, w)
            r["send"][:, :, cols] = y[pairs - sent :].astype(BF16)
            r["kept"][:, :, cols] = y[:sent]
    r["token"][...] = jnp.zeros_like(r["token"])
    for c in stores:
        c.wait()


def step_call(static, common, out, compute=None, finish=(), place=(), after=()):
    m, pairs, sent = static["m"], static["pairs"], static["sent"]
    smem = pl.BlockSpec(memory_space=pltpu.SMEM)
    vmem = pl.BlockSpec(memory_space=pltpu.VMEM)
    anym = pl.BlockSpec(memory_space=pl.ANY)
    names, args, specs = [], [], []
    outs, shapes, ospecs = [], [], []
    snames, scratch = [], []

    def take(name, arg, spec):
        names.append(name)
        args.append(arg)
        specs.append(spec)

    def give(name, shape, dtype, spec):
        outs.append(name)
        shapes.append(jax.ShapeDtypeStruct(shape, dtype))
        ospecs.append(spec)

    def hold(name, what):
        snames.append(name)
        scratch.append(what)

    def rows_in(unit):
        return sum(block[-1] for block in unit)

    first = "meta" not in common
    if first:
        for name in ("ids", "owners", "w0", "w1"):
            take(name, common[name], smem)
        for name in ("res0", "res1"):
            take(name, common[name], vmem)
        give("meta", (1, 2 * CAP + 2), jnp.int32, smem)
        give("spread", (2 * pairs * static["nb"], LANES), F32, vmem)
        give("res", (2 * m, m), BF16, vmem)
    else:
        take("meta", common["meta"], smem)
    flops = 0
    if compute is not None:
        unit, xs = compute
        total = rows_in(unit)
        if not first:
            take("res", common["res"], vmem)
        if not first:
            take("spread", common["spread"], vmem)
        for lane, x in enumerate(xs):
            take(f"x{lane}", x, vmem)
        give("send", (sent, total, m), BF16, vmem)
        give("kept", (sent, total, m), F32, vmem)
        hold("abuf", pltpu.VMEM((pairs * total, 2 * m), BF16))
        flops += 2 * pairs * total * 2 * m * m
    for j, (unit, kept, crossed) in enumerate(finish):
        take(f"kept{j}", kept, vmem)
        take(f"crossed{j}", crossed, vmem)
        give(f"swap{j}", (CAP, rows_in(unit), m), BF16, vmem)
        hold(f"fin{j}", pltpu.VMEM((CAP, rows_in(unit), m), F32))
        hold(f"finsem{j}", pltpu.SemaphoreType.DMA((len(unit),)))
    for j, (unit, swapped) in enumerate(place):
        take(f"swapped{j}", swapped, vmem)
        hold(f"put{j}", pltpu.VMEM((CAP, rows_in(unit), m), F32))
        hold(f"putsem{j}", pltpu.SemaphoreType.DMA((len(unit),)))
    for j, x in enumerate(after):
        take(f"after{j}", x, anym)
    give("token", (8, LANES), F32, vmem)
    aliases = {}
    if finish or place:
        give("out", (CAP, m, m), F32, anym)
        if out is not None:
            aliases[len(names)] = outs.index("out")
            take("out_in", out, anym)
    cfg = dict(
        static,
        first=first,
        compute=None if compute is None else compute[0],
        finish=[f[0] for f in finish],
        place=[p[0] for p in place],
        tiles=4,
        names=names + outs + snames,
    )
    got = pl.pallas_call(
        functools.partial(step_kernel, cfg),
        in_specs=specs,
        out_specs=ospecs,
        out_shape=shapes,
        scratch_shapes=scratch,
        input_output_aliases=aliases,
        compiler_params=pltpu.CompilerParams(vmem_limit_bytes=24 * 1024 * 1024),
        cost_estimate=pl.CostEstimate(flops=KERNEL_COST, bytes_accessed=1000, transcendentals=0),
    )(*args)
    return dict(zip(outs, got, strict=True))


def shards(broadcast_ops, resident_ops, integrals, owner_list):
    n_sector = lax.axis_size("sector")
    n_owner = lax.axis_size("owner")
    sector = lax.axis_index("sector")
    owner = lax.axis_index("owner")
    nb, rows, m = broadcast_ops.shape[1:]
    pairs = owner_list.shape[1]
    half = rows // 2
    core = sector % 2
    swap_core = [(i, i ^ 1) for i in range(n_sector)]
    swap_side = [(i, (i + 2) % n_sector) for i in range(n_sector)]
    order = ring_order(n_owner)
    up = [(order[i], order[(i + 1) % n_owner]) for i in range(n_owner)]
    down = [(b, a) for a, b in up]
    if half % 32 == 0:
        lanes = [(1, 0, half // 2), (-1, half // 2, half // 2)]
    else:
        lanes = [(1, 0, half)]
    cuts = 2 if lanes[0][2] % 32 == 0 else 1
    static = dict(m=m, nb=nb, half=half, n_owner=n_owner, pairs=pairs, sent=min(pairs, CAP + 1))

    shared = broadcast_ops[0]
    theirs = lax.dynamic_slice_in_dim(shared, (1 - core) * half, half, 1).astype(BF16)
    arrived = lax.ppermute(theirs, "sector", swap_core)
    mine = lax.dynamic_slice_in_dim(shared, core * half, half, 1).astype(BF16)
    xs = [jnp.stack([mine[:, a : a + n], arrived[:, a : a + n]]) for _, a, n in lanes]
    resident, *xs = lax.optimization_barrier((resident_ops[0, 0], *xs))
    res_own = resident.astype(BF16)
    w_own = integrals[0, 0]
    w_other = lax.ppermute(w_own, "sector", swap_core)
    res_other = lax.ppermute(res_own, "sector", swap_core)
    q = jnp.where(owner % 2 == 0, owner // 2, n_owner - 1 - owner // 2)
    ids = jnp.stack([sector // 2, core, q]).astype(jnp.int32)
    common = {"ids": ids, "owners": owner_list, "w0": w_own, "w1": w_other, "res0": res_own, "res1": res_other}

    def send_on(x, turn):
        return lax.ppermute(x, "owner", up if turn == 1 else down)

    units, kept, crossed, swapped = [], {}, {}, {}
    to_finish, to_place = [], []
    state = {"out": None, "token": None}

    def call(unit, rows, n_finish, n_place):
        finish = [to_finish.pop(0) for _ in range(max(0, n_finish))]
        place = [to_place.pop(0) for _ in range(max(0, n_place))]
        got = step_call(
            static,
            common,
            state["out"],
            None if unit is None else (unit, rows),
            [(units[f], kept[f], crossed[f]) for f in finish],
            [(units[p], swapped[p]) for p in place],
            [] if state["token"] is None else [state["token"]],
        )
        common.update({name: got[name] for name in ("meta", "spread", "res") if name in got})
        state["out"], state["token"] = got.get("out", state["out"]), got["token"]
        if unit is not None:
            i = len(units)
            units.append(unit)
            kept[i] = got["kept"]
            crossed[i] = lax.ppermute(got["send"], "sector", swap_side)
            to_finish.append(i)
        for j, f in enumerate(finish):
            swapped[f] = lax.ppermute(got[f"swap{j}"], "sector", swap_core)
            to_place.append(f)

    last = n_owner - 1
    for step in range(last):
        unit = [(step, *lane) for lane in lanes]
        if state["token"] is not None:
            for i in range(len(xs) - 1, -1, -1):
                xs[i], state["token"] = lax.optimization_barrier((xs[i], state["token"]))
        if step < last - 1:
            then = [send_on(x, lane[0]) for x, lane in zip(xs, lanes, strict=True)]
        else:
            cut = [jnp.split(x, cuts, 2) for x in xs]
            then = [[send_on(x[0], lane[0]) for x, lane in zip(cut, lanes, strict=True)]]
        if step < last - 1:
            call(unit, xs, len(to_finish) - FINISH_LAG, len(to_place) - PLACE_LAG)
            xs = then
        else:
            call(unit, xs, 0, 0)
            for c in range(1, cuts):
                for x in cut:
                    x[c], state["token"] = lax.optimization_barrier((x[c], state["token"]))
                then.append([send_on(x[c], lane[0]) for x, lane in zip(cut, lanes, strict=True)])
            xs = then
    for c in range(cuts):
        unit = [(last, turn, start + c * (rows // cuts), rows // cuts) for turn, start, rows in lanes]
        if c < cuts - 1:
            call(unit, xs[c], len(to_finish) - 1, len(to_place))
        else:
            call(unit, xs[c], len(to_finish) - 1, 0)
    call(None, None, len(to_finish) - 1, len(to_place) - 1)
    call(None, None, 1, 1)
    call(None, None, 0, len(to_place))
    return state["out"][None, None]


def solution(mesh):
    in_specs = (
        P("sector", None, "owner", None),
        P("sector", "owner", None, None),
        P("sector", "owner", None, None),
        P("owner", None),
    )
    out_specs = P("sector", "owner", None, None, None)
    return jax.shard_map(shards, mesh=mesh, in_specs=in_specs, out_specs=out_specs, check_vma=False)
```

```python
import functools

import jax
import jax.numpy as jnp
from jax import lax
from jax.experimental import pallas as pl
from jax.experimental.pallas import tpu as pltpu
from jax.sharding import PartitionSpec as P

CAP = 2
KERNEL_COST = 3 * 10**9
FINISH_LAG = 1
PLACE_LAG = 0
LANES = 128
BF16 = jnp.bfloat16
F32 = jnp.float32


def ring_order(n):
    return list(range(0, n, 2)) + list(range(1, n, 2))[::-1]


def plan_of(owners_ref, side):
    n = owners_ref.shape[1]
    own = [owners_ref[0, p] for p in range(n)]
    rank, key = [], []
    for p in range(n):
        r = jnp.int32(0)
        for q in range(p):
            r = r + (own[q] == own[p]).astype(jnp.int32)
        rank.append(r)
        key.append(own[p] * CAP + r)
    place = []
    for p in range(n):
        r = jnp.int32(0)
        for q in range(n):
            if q != p:
                r = r + (key[q] < key[p]).astype(jnp.int32)
        place.append(jnp.where(side == 0, r, n - 1 - r))
    pair_at = []
    for i in range(n):
        r = jnp.int32(0)
        for p in range(n):
            r = r + jnp.where(place[p] == i, p, 0)
        pair_at.append(r)

    def slot_place(sector, slot):
        r = jnp.int32(-1)
        for p in range(n):
            r = jnp.where((own[p] == sector) & (rank[p] == slot), place[p], r)
        return r

    return pair_at, slot_place


def prepare(r, m):
    ids, meta, spread = r["ids"], r["meta"], r["spread"]
    side, core = ids[0], ids[1]
    pair_at, slot_place = plan_of(r["owners"], side)
    for slot in range(CAP):
        meta[0, slot] = slot_place(side * 2 + core, slot)
        meta[0, CAP + slot] = slot_place(side * 2 + 1 - core, slot)
    meta[0, 2 * CAP] = core
    meta[0, 2 * CAP + 1] = ids[2]
    for s in range(2):
        w = r[f"w{s}"]
        nb = w.shape[1]
        for i, pair in enumerate(pair_at):
            for k in range(nb):
                row = (s * len(pair_at) + i) * nb + k
                spread[pl.ds(row, 1), :] = jnp.full((1, LANES), w[pair, k], F32)
        r["res"][pl.ds(s * m, m), :] = r[f"res{s}"][...]


def step_kernel(cfg, *refs):
    r = dict(zip(cfg["names"], refs, strict=True))
    half, n_owner, m, nb = cfg["half"], cfg["n_owner"], cfg["m"], cfg["nb"]
    pairs, sent = cfg["pairs"], cfg["sent"]
    if cfg["first"]:
        prepare(r, m)
    place_of = [r["meta"][0, slot] for slot in range(CAP)]
    other_of = [r["meta"][0, CAP + slot] for slot in range(CAP)]
    core, q = r["meta"][0, 2 * CAP], r["meta"][0, 2 * CAP + 1]
    stores = []

    def store(buf, sem, unit, which):
        base = 0
        for lane, (step, turn, start, rows) in enumerate(unit):
            at = lax.rem(q - turn * step + 2 * n_owner, n_owner)
            owner = jnp.where(at < n_owner // 2, 2 * at, 2 * (n_owner - 1 - at) + 1)
            row = pl.multiple_of(owner * (2 * half) + which * half + start, 8)
            c = pltpu.make_async_copy(
                r[buf].at[:, pl.ds(base, rows), :], r["out"].at[:, pl.ds(row, rows), :], r[sem].at[lane]
            )
            c.start()
            stores.append(c)
            base += rows

    for j, unit in enumerate(cfg["finish"]):
        kept, crossed, fin = r[f"kept{j}"], r[f"crossed{j}"], r[f"fin{j}"]
        for slot in range(CAP):
            i = jnp.maximum(other_of[slot], 0)
            r[f"swap{j}"][slot] = (kept[i] + crossed[sent - 1 - i].astype(F32)).astype(BF16)
        for slot in range(CAP):
            place = place_of[slot]
            i = jnp.maximum(place, 0)
            fin[slot] = jnp.where(place >= 0, kept[i] + crossed[sent - 1 - i].astype(F32), 0.0)
        store(f"fin{j}", f"finsem{j}", unit, core)
    for j, unit in enumerate(cfg["place"]):
        for slot in range(CAP):
            v = r[f"swapped{j}"][slot].astype(F32)
            r[f"put{j}"][slot] = jnp.where(place_of[slot] >= 0, v, 0.0)
        store(f"put{j}", f"putsem{j}", unit, 1 - core)

    if cfg["compute"] is not None:
        unit = cfg["compute"]
        total = sum(block[-1] for block in unit)
        for s in range(2):
            base = 0
            for lane, (*_, rows) in enumerate(unit):
                for c in range(0, m, LANES):
                    cols = pl.ds(c, LANES)
                    x = [r[f"x{lane}"][s, k, :, cols].astype(F32) for k in range(nb)]
                    for i in range(pairs):
                        row = (s * pairs + i) * nb
                        a = r["spread"][pl.ds(row, 1), :] * x[0]
                        for k in range(1, nb):
                            a = a + r["spread"][pl.ds(row + k, 1), :] * x[k]
                        r["abuf"][pl.ds(i * total + base, rows), pl.ds(s * m + c, LANES)] = a.astype(BF16)
                base += rows
        w = m // cfg["tiles"]
        for t in range(cfg["tiles"]):
            cols = pl.ds(t * w, w)
            y = jnp.dot(r["abuf"][...], r["res"][:, cols], preferred_element_type=F32)
            y = y.reshape(pairs, total, w)
            r["send"][:, :, cols] = y[pairs - sent :].astype(BF16)
            r["kept"][:, :, cols] = y[:sent]
    r["token"][...] = jnp.zeros_like(r["token"])
    for c in stores:
        c.wait()


def step_call(static, common, out, compute=None, finish=(), place=(), after=()):
    m, pairs, sent = static["m"], static["pairs"], static["sent"]
    smem = pl.BlockSpec(memory_space=pltpu.SMEM)
    vmem = pl.BlockSpec(memory_space=pltpu.VMEM)
    anym = pl.BlockSpec(memory_space=pl.ANY)
    names, args, specs = [], [], []
    outs, shapes, ospecs = [], [], []
    snames, scratch = [], []

    def take(name, arg, spec):
        names.append(name)
        args.append(arg)
        specs.append(spec)

    def give(name, shape, dtype, spec):
        outs.append(name)
        shapes.append(jax.ShapeDtypeStruct(shape, dtype))
        ospecs.append(spec)

    def hold(name, what):
        snames.append(name)
        scratch.append(what)

    def rows_in(unit):
        return sum(block[-1] for block in unit)

    first = "meta" not in common
    if first:
        for name in ("ids", "owners", "w0", "w1"):
            take(name, common[name], smem)
        for name in ("res0", "res1"):
            take(name, common[name], vmem)
        give("meta", (1, 2 * CAP + 2), jnp.int32, smem)
        give("spread", (2 * pairs * static["nb"], LANES), F32, vmem)
        give("res", (2 * m, m), BF16, vmem)
    else:
        take("meta", common["meta"], smem)
    flops = 0
    if compute is not None:
        unit, xs = compute
        total = rows_in(unit)
        if not first:
            take("res", common["res"], vmem)
        if not first:
            take("spread", common["spread"], vmem)
        for lane, x in enumerate(xs):
            take(f"x{lane}", x, vmem)
        give("send", (sent, total, m), BF16, vmem)
        give("kept", (sent, total, m), F32, vmem)
        hold("abuf", pltpu.VMEM((pairs * total, 2 * m), BF16))
        flops += 2 * pairs * total * 2 * m * m
    for j, (unit, kept, crossed) in enumerate(finish):
        take(f"kept{j}", kept, vmem)
        take(f"crossed{j}", crossed, vmem)
        give(f"swap{j}", (CAP, rows_in(unit), m), BF16, vmem)
        hold(f"fin{j}", pltpu.VMEM((CAP, rows_in(unit), m), F32))
        hold(f"finsem{j}", pltpu.SemaphoreType.DMA((len(unit),)))
    for j, (unit, swapped) in enumerate(place):
        take(f"swapped{j}", swapped, vmem)
        hold(f"put{j}", pltpu.VMEM((CAP, rows_in(unit), m), F32))
        hold(f"putsem{j}", pltpu.SemaphoreType.DMA((len(unit),)))
    for j, x in enumerate(after):
        take(f"after{j}", x, anym)
    give("token", (8, LANES), F32, vmem)
    aliases = {}
    if finish or place:
        give("out", (CAP, m, m), F32, anym)
        if out is not None:
            aliases[len(names)] = outs.index("out")
            take("out_in", out, anym)
    cfg = dict(
        static,
        first=first,
        compute=None if compute is None else compute[0],
        finish=[f[0] for f in finish],
        place=[p[0] for p in place],
        tiles=4,
        names=names + outs + snames,
    )
    got = pl.pallas_call(
        functools.partial(step_kernel, cfg),
        in_specs=specs,
        out_specs=ospecs,
        out_shape=shapes,
        scratch_shapes=scratch,
        input_output_aliases=aliases,
        compiler_params=pltpu.CompilerParams(vmem_limit_bytes=24 * 1024 * 1024),
        cost_estimate=pl.CostEstimate(flops=KERNEL_COST, bytes_accessed=1000, transcendentals=0),
    )(*args)
    return dict(zip(outs, got, strict=True))


def shards(broadcast_ops, resident_ops, integrals, owner_list):
    n_sector = lax.axis_size("sector")
    n_owner = lax.axis_size("owner")
    sector = lax.axis_index("sector")
    owner = lax.axis_index("owner")
    nb, rows, m = broadcast_ops.shape[1:]
    pairs = owner_list.shape[1]
    half = rows // 2
    core = sector % 2
    swap_core = [(i, i ^ 1) for i in range(n_sector)]
    swap_side = [(i, (i + 2) % n_sector) for i in range(n_sector)]
    order = ring_order(n_owner)
    up = [(order[i], order[(i + 1) % n_owner]) for i in range(n_owner)]
    down = [(b, a) for a, b in up]
    if half % 32 == 0:
        lanes = [(1, 0, half // 2), (-1, half // 2, half // 2)]
    else:
        lanes = [(1, 0, half)]
    cuts = 2 if lanes[0][2] % 32 == 0 else 1
    static = dict(m=m, nb=nb, half=half, n_owner=n_owner, pairs=pairs, sent=min(pairs, CAP + 1))

    shared = broadcast_ops[0]
    theirs = lax.dynamic_slice_in_dim(shared, (1 - core) * half, half, 1).astype(BF16)
    arrived = lax.ppermute(theirs, "sector", swap_core)
    mine = lax.dynamic_slice_in_dim(shared, core * half, half, 1).astype(BF16)
    xs = [jnp.stack([mine[:, a : a + n], arrived[:, a : a + n]]) for _, a, n in lanes]
    resident, *xs = lax.optimization_barrier((resident_ops[0, 0], *xs))
    res_own = resident.astype(BF16)
    w_own = integrals[0, 0]
    w_other = lax.ppermute(w_own, "sector", swap_core)
    res_other = lax.ppermute(res_own, "sector", swap_core)
    q = jnp.where(owner % 2 == 0, owner // 2, n_owner - 1 - owner // 2)
    ids = jnp.stack([sector // 2, core, q]).astype(jnp.int32)
    common = {"ids": ids, "owners": owner_list, "w0": w_own, "w1": w_other, "res0": res_own, "res1": res_other}

    def send_on(x, turn):
        return lax.ppermute(x, "owner", up if turn == 1 else down)

    units, kept, crossed, swapped = [], {}, {}, {}
    to_finish, to_place = [], []
    state = {"out": None, "token": None}

    def call(unit, rows, n_finish, n_place, after=()):
        finish = [to_finish.pop(0) for _ in range(max(0, n_finish))]
        place = [to_place.pop(0) for _ in range(max(0, n_place))]
        got = step_call(
            static,
            common,
            state["out"],
            None if unit is None else (unit, rows),
            [(units[f], kept[f], crossed[f]) for f in finish],
            [(units[p], swapped[p]) for p in place],
            [*after] if state["token"] is None else [state["token"], *after],
        )
        common.update({name: got[name] for name in ("meta", "spread", "res") if name in got})
        state["out"], state["token"] = got.get("out", state["out"]), got["token"]
        if unit is not None:
            i = len(units)
            units.append(unit)
            kept[i] = got["kept"]
            crossed[i] = lax.ppermute(got["send"], "sector", swap_side)
            to_finish.append(i)
        for j, f in enumerate(finish):
            swapped[f] = lax.ppermute(got[f"swap{j}"], "sector", swap_core)
            to_place.append(f)

    last = n_owner - 1
    for step in range(last):
        unit = [(step, *lane) for lane in lanes]
        if state["token"] is not None:
            for i in range(len(xs) - 1, -1, -1):
                xs[i], state["token"] = lax.optimization_barrier((xs[i], state["token"]))
        if step < last - 1:
            then = [send_on(x, lane[0]) for x, lane in zip(xs, lanes, strict=True)]
        else:
            cut = [jnp.split(x, cuts, 2) for x in xs]
            then = [[send_on(x[0], lane[0]) for x, lane in zip(cut, lanes, strict=True)]]
        if step < last - 1:
            call(unit, xs, len(to_finish) - FINISH_LAG, len(to_place) - PLACE_LAG)
            xs = then
        else:
            call(unit, xs, 0, 0)
            for c in range(1, cuts):
                for x in cut:
                    x[c], state["token"] = lax.optimization_barrier((x[c], state["token"]))
                then.append([send_on(x[c], lane[0]) for x, lane in zip(cut, lanes, strict=True)])
            xs = then
    for c in range(cuts):
        unit = [(last, turn, start + c * (rows // cuts), rows // cuts) for turn, start, rows in lanes]
        if c < cuts - 1:
            call(unit, xs[c], len(to_finish) - 1, len(to_place))
        else:
            call(unit, xs[c], 0, 0, [crossed[i] for i in to_finish[:-1]])
    call(None, None, len(to_finish) - 1, len(to_place))
    call(None, None, 1, 0)
    call(None, None, 0, len(to_place) - 1)
    call(None, None, 0, 1)
    return state["out"][None, None]


def solution(mesh):
    in_specs = (
        P("sector", None, "owner", None),
        P("sector", "owner", None, None),
        P("sector", "owner", None, None),
        P("owner", None),
    )
    out_specs = P("sector", "owner", None, None, None)
    return jax.shard_map(shards, mesh=mesh, in_specs=in_specs, out_specs=out_specs, check_vma=False)
```

```python
import functools

import jax
import jax.numpy as jnp
from jax import lax
from jax.experimental import pallas as pl
from jax.experimental.pallas import tpu as pltpu
from jax.sharding import PartitionSpec as P

CAP = 2
KERNEL_COST = 3 * 10**9
FINISH_LAG = 1
PLACE_LAG = 0
LANES = 128
BF16 = jnp.bfloat16
F32 = jnp.float32


def ring_order(n):
    return list(range(0, n, 2)) + list(range(1, n, 2))[::-1]


def plan_of(owners_ref, side):
    n = owners_ref.shape[1]
    own = [owners_ref[0, p] for p in range(n)]
    rank, key = [], []
    for p in range(n):
        r = jnp.int32(0)
        for q in range(p):
            r = r + (own[q] == own[p]).astype(jnp.int32)
        rank.append(r)
        key.append(own[p] * CAP + r)
    place = []
    for p in range(n):
        r = jnp.int32(0)
        for q in range(n):
            if q != p:
                r = r + (key[q] < key[p]).astype(jnp.int32)
        place.append(jnp.where(side == 0, r, n - 1 - r))
    pair_at = []
    for i in range(n):
        r = jnp.int32(0)
        for p in range(n):
            r = r + jnp.where(place[p] == i, p, 0)
        pair_at.append(r)

    def slot_place(sector, slot):
        r = jnp.int32(-1)
        for p in range(n):
            r = jnp.where((own[p] == sector) & (rank[p] == slot), place[p], r)
        return r

    return pair_at, slot_place


def prepare(r, m):
    ids, meta, spread = r["ids"], r["meta"], r["spread"]
    side, core = ids[0], ids[1]
    pair_at, slot_place = plan_of(r["owners"], side)
    for slot in range(CAP):
        meta[0, slot] = slot_place(side * 2 + core, slot)
        meta[0, CAP + slot] = slot_place(side * 2 + 1 - core, slot)
    meta[0, 2 * CAP] = core
    meta[0, 2 * CAP + 1] = ids[2]
    for s in range(2):
        w = r[f"w{s}"]
        nb = w.shape[1]
        for i, pair in enumerate(pair_at):
            for k in range(nb):
                row = (s * len(pair_at) + i) * nb + k
                spread[pl.ds(row, 1), :] = jnp.full((1, LANES), w[pair, k], F32)
        r["res"][pl.ds(s * m, m), :] = r[f"res{s}"][...]


def step_kernel(cfg, *refs):
    r = dict(zip(cfg["names"], refs, strict=True))
    half, n_owner, m, nb = cfg["half"], cfg["n_owner"], cfg["m"], cfg["nb"]
    pairs, sent = cfg["pairs"], cfg["sent"]
    if cfg["first"]:
        prepare(r, m)
    place_of = [r["meta"][0, slot] for slot in range(CAP)]
    other_of = [r["meta"][0, CAP + slot] for slot in range(CAP)]
    core, q = r["meta"][0, 2 * CAP], r["meta"][0, 2 * CAP + 1]
    stores = []

    def store(buf, sem, unit, which):
        base = 0
        for lane, (step, turn, start, rows) in enumerate(unit):
            at = lax.rem(q - turn * step + 2 * n_owner, n_owner)
            owner = jnp.where(at < n_owner // 2, 2 * at, 2 * (n_owner - 1 - at) + 1)
            row = pl.multiple_of(owner * (2 * half) + which * half + start, 8)
            c = pltpu.make_async_copy(
                r[buf].at[:, pl.ds(base, rows), :], r["out"].at[:, pl.ds(row, rows), :], r[sem].at[lane]
            )
            c.start()
            stores.append(c)
            base += rows

    for j, unit in enumerate(cfg["finish"]):
        kept, crossed, fin = r[f"kept{j}"], r[f"crossed{j}"], r[f"fin{j}"]
        for slot in range(CAP):
            i = jnp.maximum(other_of[slot], 0)
            r[f"swap{j}"][slot] = (kept[i] + crossed[sent - 1 - i].astype(F32)).astype(BF16)
        for slot in range(CAP):
            place = place_of[slot]
            i = jnp.maximum(place, 0)
            fin[slot] = jnp.where(place >= 0, kept[i] + crossed[sent - 1 - i].astype(F32), 0.0)
        store(f"fin{j}", f"finsem{j}", unit, core)
    for j, unit in enumerate(cfg["place"]):
        for slot in range(CAP):
            v = r[f"swapped{j}"][slot].astype(F32)
            r[f"put{j}"][slot] = jnp.where(place_of[slot] >= 0, v, 0.0)
        store(f"put{j}", f"putsem{j}", unit, 1 - core)

    if cfg["compute"] is not None:
        unit = cfg["compute"]
        total = sum(block[-1] for block in unit)
        for s in range(2):
            base = 0
            for lane, (*_, rows) in enumerate(unit):
                for c in range(0, m, LANES):
                    cols = pl.ds(c, LANES)
                    x = [r[f"x{lane}"][s, k, :, cols].astype(F32) for k in range(nb)]
                    for i in range(pairs):
                        row = (s * pairs + i) * nb
                        a = r["spread"][pl.ds(row, 1), :] * x[0]
                        for k in range(1, nb):
                            a = a + r["spread"][pl.ds(row + k, 1), :] * x[k]
                        r["abuf"][pl.ds(i * total + base, rows), pl.ds(s * m + c, LANES)] = a.astype(BF16)
                base += rows
        w = m // cfg["tiles"]
        for t in range(cfg["tiles"]):
            cols = pl.ds(t * w, w)
            y = jnp.dot(r["abuf"][...], r["res"][:, cols], preferred_element_type=F32)
            y = y.reshape(pairs, total, w)
            r["send"][:, :, cols] = y[pairs - sent :].astype(BF16)
            r["kept"][:, :, cols] = y[:sent]
    if cfg["compute"] is not None:
        r["token"][...] = jnp.zeros_like(r["token"])
    for c in stores:
        c.wait()


def step_call(static, common, out, compute=None, finish=(), place=(), after=()):
    m, pairs, sent = static["m"], static["pairs"], static["sent"]
    smem = pl.BlockSpec(memory_space=pltpu.SMEM)
    vmem = pl.BlockSpec(memory_space=pltpu.VMEM)
    anym = pl.BlockSpec(memory_space=pl.ANY)
    names, args, specs = [], [], []
    outs, shapes, ospecs = [], [], []
    snames, scratch = [], []

    def take(name, arg, spec):
        names.append(name)
        args.append(arg)
        specs.append(spec)

    def give(name, shape, dtype, spec):
        outs.append(name)
        shapes.append(jax.ShapeDtypeStruct(shape, dtype))
        ospecs.append(spec)

    def hold(name, what):
        snames.append(name)
        scratch.append(what)

    def rows_in(unit):
        return sum(block[-1] for block in unit)

    first = "meta" not in common
    if first:
        for name in ("ids", "owners", "w0", "w1"):
            take(name, common[name], smem)
        for name in ("res0", "res1"):
            take(name, common[name], vmem)
        give("meta", (1, 2 * CAP + 2), jnp.int32, smem)
        give("spread", (2 * pairs * static["nb"], LANES), F32, vmem)
        give("res", (2 * m, m), BF16, vmem)
    else:
        take("meta", common["meta"], smem)
    flops = 0
    if compute is not None:
        unit, xs = compute
        total = rows_in(unit)
        if not first:
            take("res", common["res"], vmem)
        if not first:
            take("spread", common["spread"], vmem)
        for lane, x in enumerate(xs):
            take(f"x{lane}", x, vmem)
        give("send", (sent, total, m), BF16, vmem)
        give("kept", (sent, total, m), F32, vmem)
        hold("abuf", pltpu.VMEM((pairs * total, 2 * m), BF16))
        flops += 2 * pairs * total * 2 * m * m
    for j, (unit, kept, crossed) in enumerate(finish):
        take(f"kept{j}", kept, vmem)
        take(f"crossed{j}", crossed, vmem)
        give(f"swap{j}", (CAP, rows_in(unit), m), BF16, vmem)
        hold(f"fin{j}", pltpu.VMEM((CAP, rows_in(unit), m), F32))
        hold(f"finsem{j}", pltpu.SemaphoreType.DMA((len(unit),)))
    for j, (unit, swapped) in enumerate(place):
        take(f"swapped{j}", swapped, vmem)
        hold(f"put{j}", pltpu.VMEM((CAP, rows_in(unit), m), F32))
        hold(f"putsem{j}", pltpu.SemaphoreType.DMA((len(unit),)))
    for j, x in enumerate(after):
        take(f"after{j}", x, anym)
    if compute is not None:
        give("token", (8, LANES), F32, vmem)
    aliases = {}
    if finish or place:
        give("out", (CAP, m, m), F32, anym)
        if out is not None:
            aliases[len(names)] = outs.index("out")
            take("out_in", out, anym)
    cfg = dict(
        static,
        first=first,
        compute=None if compute is None else compute[0],
        finish=[f[0] for f in finish],
        place=[p[0] for p in place],
        tiles=4,
        names=names + outs + snames,
    )
    got = pl.pallas_call(
        functools.partial(step_kernel, cfg),
        in_specs=specs,
        out_specs=ospecs,
        out_shape=shapes,
        scratch_shapes=scratch,
        input_output_aliases=aliases,
        compiler_params=pltpu.CompilerParams(vmem_limit_bytes=24 * 1024 * 1024),
        cost_estimate=pl.CostEstimate(flops=KERNEL_COST, bytes_accessed=1000, transcendentals=0),
    )(*args)
    return dict(zip(outs, got, strict=True))


def shards(broadcast_ops, resident_ops, integrals, owner_list):
    n_sector = lax.axis_size("sector")
    n_owner = lax.axis_size("owner")
    sector = lax.axis_index("sector")
    owner = lax.axis_index("owner")
    nb, rows, m = broadcast_ops.shape[1:]
    pairs = owner_list.shape[1]
    half = rows // 2
    core = sector % 2
    swap_core = [(i, i ^ 1) for i in range(n_sector)]
    swap_side = [(i, (i + 2) % n_sector) for i in range(n_sector)]
    order = ring_order(n_owner)
    up = [(order[i], order[(i + 1) % n_owner]) for i in range(n_owner)]
    down = [(b, a) for a, b in up]
    if half % 32 == 0:
        lanes = [(1, 0, half // 2), (-1, half // 2, half // 2)]
    else:
        lanes = [(1, 0, half)]
    cuts = 2 if lanes[0][2] % 32 == 0 else 1
    static = dict(m=m, nb=nb, half=half, n_owner=n_owner, pairs=pairs, sent=min(pairs, CAP + 1))

    shared = broadcast_ops[0]
    theirs = lax.dynamic_slice_in_dim(shared, (1 - core) * half, half, 1).astype(BF16)
    arrived = lax.ppermute(theirs, "sector", swap_core)
    mine = lax.dynamic_slice_in_dim(shared, core * half, half, 1).astype(BF16)
    xs = [jnp.stack([mine[:, a : a + n], arrived[:, a : a + n]]) for _, a, n in lanes]
    resident, *xs = lax.optimization_barrier((resident_ops[0, 0], *xs))
    res_own = resident.astype(BF16)
    w_own = integrals[0, 0]
    w_other = lax.ppermute(w_own, "sector", swap_core)
    res_other = lax.ppermute(res_own, "sector", swap_core)
    q = jnp.where(owner % 2 == 0, owner // 2, n_owner - 1 - owner // 2)
    ids = jnp.stack([sector // 2, core, q]).astype(jnp.int32)
    common = {"ids": ids, "owners": owner_list, "w0": w_own, "w1": w_other, "res0": res_own, "res1": res_other}

    def send_on(x, turn):
        return lax.ppermute(x, "owner", up if turn == 1 else down)

    units, kept, crossed, swapped = [], {}, {}, {}
    to_finish, to_place = [], []
    state = {"out": None, "token": None}

    def call(unit, rows, n_finish, n_place, after=()):
        finish = [to_finish.pop(0) for _ in range(max(0, n_finish))]
        place = [to_place.pop(0) for _ in range(max(0, n_place))]
        got = step_call(
            static,
            common,
            state["out"],
            None if unit is None else (unit, rows),
            [(units[f], kept[f], crossed[f]) for f in finish],
            [(units[p], swapped[p]) for p in place],
            [*after] if state["token"] is None else [state["token"], *after],
        )
        common.update({name: got[name] for name in ("meta", "spread", "res") if name in got})
        state["out"], state["token"] = got.get("out", state["out"]), got.get("token")
        if unit is not None:
            i = len(units)
            units.append(unit)
            kept[i] = got["kept"]
            crossed[i] = lax.ppermute(got["send"], "sector", swap_side)
            to_finish.append(i)
        for j, f in enumerate(finish):
            swapped[f] = lax.ppermute(got[f"swap{j}"], "sector", swap_core)
            to_place.append(f)

    last = n_owner - 1
    for step in range(last):
        unit = [(step, *lane) for lane in lanes]
        if state["token"] is not None:
            for i in range(len(xs) - 1, -1, -1):
                xs[i], state["token"] = lax.optimization_barrier((xs[i], state["token"]))
        if step < last - 1:
            then = [send_on(x, lane[0]) for x, lane in zip(xs, lanes, strict=True)]
        else:
            cut = [jnp.split(x, cuts, 2) for x in xs]
            then = [[send_on(x[0], lane[0]) for x, lane in zip(cut, lanes, strict=True)]]
        if step < last - 1:
            call(unit, xs, len(to_finish) - FINISH_LAG, len(to_place) - PLACE_LAG)
            xs = then
        else:
            call(unit, xs, 0, 0)
            for c in range(1, cuts):
                for x in cut:
                    x[c], state["token"] = lax.optimization_barrier((x[c], state["token"]))
                then.append([send_on(x[c], lane[0]) for x, lane in zip(cut, lanes, strict=True)])
            xs = then
    for c in range(cuts):
        unit = [(last, turn, start + c * (rows // cuts), rows // cuts) for turn, start, rows in lanes]
        if c < cuts - 1:
            call(unit, xs[c], len(to_finish) - 1, len(to_place))
        else:
            call(unit, xs[c], 0, 0, [crossed[i] for i in to_finish[:-1]])
    call(None, None, len(to_finish) - 1, len(to_place))
    call(None, None, 1, 0)
    call(None, None, 0, len(to_place) - 1)
    call(None, None, 0, 1)
    return state["out"][None, None]


def solution(mesh):
    in_specs = (
        P("sector", None, "owner", None),
        P("sector", "owner", None, None),
        P("sector", "owner", None, None),
        P("owner", None),
    )
    out_specs = P("sector", "owner", None, None, None)
    return jax.shard_map(shards, mesh=mesh, in_specs=in_specs, out_specs=out_specs, check_vma=False)
```

```python
import functools

import jax
import jax.numpy as jnp
from jax import lax
from jax.experimental import pallas as pl
from jax.experimental.pallas import tpu as pltpu
from jax.sharding import PartitionSpec as P

CAP = 2
KERNEL_COST = 3 * 10**9
FINISH_LAG = 1
PLACE_LAG = 0
LANES = 128
BF16 = jnp.bfloat16
F32 = jnp.float32


def ring_order(n):
    return list(range(0, n, 2)) + list(range(1, n, 2))[::-1]


def plan_of(owners_ref, side):
    n = owners_ref.shape[1]
    own = [owners_ref[0, p] for p in range(n)]
    rank, key = [], []
    for p in range(n):
        r = jnp.int32(0)
        for q in range(p):
            r = r + (own[q] == own[p]).astype(jnp.int32)
        rank.append(r)
        key.append(own[p] * CAP + r)
    place = []
    for p in range(n):
        r = jnp.int32(0)
        for q in range(n):
            if q != p:
                r = r + (key[q] < key[p]).astype(jnp.int32)
        place.append(jnp.where(side == 0, r, n - 1 - r))
    pair_at = []
    for i in range(n):
        r = jnp.int32(0)
        for p in range(n):
            r = r + jnp.where(place[p] == i, p, 0)
        pair_at.append(r)

    def slot_place(sector, slot):
        r = jnp.int32(-1)
        for p in range(n):
            r = jnp.where((own[p] == sector) & (rank[p] == slot), place[p], r)
        return r

    return pair_at, slot_place


def prepare(r, m):
    ids, meta, spread = r["ids"], r["meta"], r["spread"]
    side, core = ids[0], ids[1]
    pair_at, slot_place = plan_of(r["owners"], side)
    for slot in range(CAP):
        meta[0, slot] = slot_place(side * 2 + core, slot)
        meta[0, CAP + slot] = slot_place(side * 2 + 1 - core, slot)
    meta[0, 2 * CAP] = core
    meta[0, 2 * CAP + 1] = ids[2]
    for s in range(2):
        w = r[f"w{s}"]
        nb = w.shape[1]
        for i, pair in enumerate(pair_at):
            for k in range(nb):
                row = (s * len(pair_at) + i) * nb + k
                spread[pl.ds(row, 1), :] = jnp.full((1, LANES), w[pair, k], F32)
        r["res"][pl.ds(s * m, m), :] = r[f"res{s}"][...]


def step_kernel(cfg, *refs):
    r = dict(zip(cfg["names"], refs, strict=True))
    half, n_owner, m, nb = cfg["half"], cfg["n_owner"], cfg["m"], cfg["nb"]
    pairs, sent = cfg["pairs"], cfg["sent"]
    if cfg["first"]:
        prepare(r, m)
    place_of = [r["meta"][0, slot] for slot in range(CAP)]
    other_of = [r["meta"][0, CAP + slot] for slot in range(CAP)]
    core, q = r["meta"][0, 2 * CAP], r["meta"][0, 2 * CAP + 1]
    stores = []

    def store(buf, sem, unit, which):
        base = 0
        for lane, (step, turn, start, rows) in enumerate(unit):
            at = lax.rem(q - turn * step + 2 * n_owner, n_owner)
            owner = jnp.where(at < n_owner // 2, 2 * at, 2 * (n_owner - 1 - at) + 1)
            row = pl.multiple_of(owner * (2 * half) + which * half + start, 8)
            c = pltpu.make_async_copy(
                r[buf].at[:, pl.ds(base, rows), :], r["out"].at[:, pl.ds(row, rows), :], r[sem].at[lane]
            )
            c.start()
            stores.append(c)
            base += rows

    for j, unit in enumerate(cfg["finish"]):
        kept, crossed, fin = r[f"kept{j}"], r[f"crossed{j}"], r[f"fin{j}"]
        for slot in range(CAP):
            i = jnp.maximum(other_of[slot], 0)
            r[f"swap{j}"][slot] = (kept[i] + crossed[sent - 1 - i].astype(F32)).astype(BF16)
        for slot in range(CAP):
            place = place_of[slot]
            i = jnp.maximum(place, 0)
            fin[slot] = jnp.where(place >= 0, kept[i] + crossed[sent - 1 - i].astype(F32), 0.0)
        store(f"fin{j}", f"finsem{j}", unit, core)
    for j, unit in enumerate(cfg["place"]):
        for slot in range(CAP):
            v = r[f"swapped{j}"][slot].astype(F32)
            r[f"put{j}"][slot] = jnp.where(place_of[slot] >= 0, v, 0.0)
        store(f"put{j}", f"putsem{j}", unit, 1 - core)

    if cfg["compute"] is not None:
        unit = cfg["compute"]
        total = sum(block[-1] for block in unit)
        for s in range(2):
            base = 0
            for lane, (*_, rows) in enumerate(unit):
                for c in range(0, m, LANES):
                    cols = pl.ds(c, LANES)
                    x = [r[f"x{lane}"][s, k, :, cols].astype(F32) for k in range(nb)]
                    for i in range(pairs):
                        row = (s * pairs + i) * nb
                        a = r["spread"][pl.ds(row, 1), :] * x[0]
                        for k in range(1, nb):
                            a = a + r["spread"][pl.ds(row + k, 1), :] * x[k]
                        r["abuf"][pl.ds(i * total + base, rows), pl.ds(s * m + c, LANES)] = a.astype(BF16)
                base += rows
        w = m // cfg["tiles"]
        for t in range(cfg["tiles"]):
            cols = pl.ds(t * w, w)
            y = jnp.dot(r["abuf"][...], r["res"][:, cols], preferred_element_type=F32)
            y = y.reshape(pairs, total, w)
            r["send"][:, :, cols] = y[pairs - sent :].astype(BF16)
            r["kept"][:, :, cols] = y[:sent]
    if cfg["compute"] is not None:
        r["token"][...] = jnp.zeros_like(r["token"])
    for c in stores:
        c.wait()


def step_call(static, common, out, compute=None, finish=(), place=(), after=()):
    m, pairs, sent = static["m"], static["pairs"], static["sent"]
    smem = pl.BlockSpec(memory_space=pltpu.SMEM)
    vmem = pl.BlockSpec(memory_space=pltpu.VMEM)
    anym = pl.BlockSpec(memory_space=pl.ANY)
    names, args, specs = [], [], []
    outs, shapes, ospecs = [], [], []
    snames, scratch = [], []

    def take(name, arg, spec):
        names.append(name)
        args.append(arg)
        specs.append(spec)

    def give(name, shape, dtype, spec):
        outs.append(name)
        shapes.append(jax.ShapeDtypeStruct(shape, dtype))
        ospecs.append(spec)

    def hold(name, what):
        snames.append(name)
        scratch.append(what)

    def rows_in(unit):
        return sum(block[-1] for block in unit)

    first = "meta" not in common
    if first:
        for name in ("ids", "owners", "w0", "w1"):
            take(name, common[name], smem)
        for name in ("res0", "res1"):
            take(name, common[name], vmem)
        give("meta", (1, 2 * CAP + 2), jnp.int32, smem)
        give("spread", (2 * pairs * static["nb"], LANES), F32, vmem)
        give("res", (2 * m, m), BF16, vmem)
    else:
        take("meta", common["meta"], smem)
    flops = 0
    if compute is not None:
        unit, xs = compute
        total = rows_in(unit)
        if not first:
            take("res", common["res"], vmem)
        if not first:
            take("spread", common["spread"], vmem)
        for lane, x in enumerate(xs):
            take(f"x{lane}", x, vmem)
        give("send", (sent, total, m), BF16, vmem)
        give("kept", (sent, total, m), F32, vmem)
        hold("abuf", pltpu.VMEM((pairs * total, 2 * m), BF16))
        flops += 2 * pairs * total * 2 * m * m
    for j, (unit, kept, crossed) in enumerate(finish):
        take(f"kept{j}", kept, vmem)
        take(f"crossed{j}", crossed, vmem)
        give(f"swap{j}", (CAP, rows_in(unit), m), BF16, vmem)
        hold(f"fin{j}", pltpu.VMEM((CAP, rows_in(unit), m), F32))
        hold(f"finsem{j}", pltpu.SemaphoreType.DMA((len(unit),)))
    for j, (unit, swapped) in enumerate(place):
        take(f"swapped{j}", swapped, vmem)
        hold(f"put{j}", pltpu.VMEM((CAP, rows_in(unit), m), F32))
        hold(f"putsem{j}", pltpu.SemaphoreType.DMA((len(unit),)))
    for j, x in enumerate(after):
        take(f"after{j}", x, anym)
    if compute is not None:
        give("token", (8, LANES), F32, vmem)
    aliases = {}
    if finish or place:
        give("out", (CAP, m, m), F32, anym)
        if out is not None:
            aliases[len(names)] = outs.index("out")
            take("out_in", out, anym)
    cfg = dict(
        static,
        first=first,
        compute=None if compute is None else compute[0],
        finish=[f[0] for f in finish],
        place=[p[0] for p in place],
        tiles=4,
        names=names + outs + snames,
    )
    got = pl.pallas_call(
        functools.partial(step_kernel, cfg),
        in_specs=specs,
        out_specs=ospecs,
        out_shape=shapes,
        scratch_shapes=scratch,
        input_output_aliases=aliases,
        compiler_params=pltpu.CompilerParams(vmem_limit_bytes=24 * 1024 * 1024),
        cost_estimate=pl.CostEstimate(flops=KERNEL_COST, bytes_accessed=1000, transcendentals=0),
    )(*args)
    return dict(zip(outs, got, strict=True))


def cast_kernel(own, shared, *refs):
    out, buf, sems = refs[-3:]
    core = lax.rem(lax.axis_index("sector"), 2)
    nb, half = out.shape[:2]
    start = pl.multiple_of((core if own else 1 - core) * half, 8)
    copies = [
        pltpu.make_async_copy(shared.at[k, pl.ds(start, half), :], buf.at[k], sems.at[k]) for k in range(nb)
    ]
    for c in copies:
        c.start()
    for k, c in enumerate(copies):
        c.wait()
        out[k] = buf[k].astype(BF16)


def cast_half(shared, own, *after):
    nb, rows, m = shared.shape
    anym = pl.BlockSpec(memory_space=pltpu.HBM)
    return pl.pallas_call(
        functools.partial(cast_kernel, own),
        in_specs=[anym] + [pl.BlockSpec(memory_space=pl.ANY)] * len(after),
        out_specs=pl.BlockSpec(memory_space=pltpu.VMEM),
        out_shape=jax.ShapeDtypeStruct((nb, rows // 2, m), BF16),
        scratch_shapes=[pltpu.VMEM((nb, rows // 2, m), F32), pltpu.SemaphoreType.DMA((nb,))],
        compiler_params=pltpu.CompilerParams(vmem_limit_bytes=50 * 1024 * 1024),
    )(shared, *after)


def shards(broadcast_ops, resident_ops, integrals, owner_list):
    n_sector = lax.axis_size("sector")
    n_owner = lax.axis_size("owner")
    sector = lax.axis_index("sector")
    owner = lax.axis_index("owner")
    nb, rows, m = broadcast_ops.shape[1:]
    pairs = owner_list.shape[1]
    half = rows // 2
    core = sector % 2
    swap_core = [(i, i ^ 1) for i in range(n_sector)]
    swap_side = [(i, (i + 2) % n_sector) for i in range(n_sector)]
    order = ring_order(n_owner)
    up = [(order[i], order[(i + 1) % n_owner]) for i in range(n_owner)]
    down = [(b, a) for a, b in up]
    if half % 32 == 0:
        lanes = [(1, 0, half // 2), (-1, half // 2, half // 2)]
    else:
        lanes = [(1, 0, half)]
    cuts = 2 if lanes[0][2] % 32 == 0 else 1
    static = dict(m=m, nb=nb, half=half, n_owner=n_owner, pairs=pairs, sent=min(pairs, CAP + 1))

    shared = broadcast_ops[0]
    theirs = cast_half(shared, False)
    arrived = lax.ppermute(theirs, "sector", swap_core)
    mine = cast_half(shared, True, theirs)
    xs = [jnp.stack([mine[:, a : a + n], arrived[:, a : a + n]]) for _, a, n in lanes]
    resident, *xs = lax.optimization_barrier((resident_ops[0, 0], *xs))
    res_own = resident.astype(BF16)
    w_own = integrals[0, 0]
    w_other = lax.ppermute(w_own, "sector", swap_core)
    res_other = lax.ppermute(res_own, "sector", swap_core)
    q = jnp.where(owner % 2 == 0, owner // 2, n_owner - 1 - owner // 2)
    ids = jnp.stack([sector // 2, core, q]).astype(jnp.int32)
    common = {"ids": ids, "owners": owner_list, "w0": w_own, "w1": w_other, "res0": res_own, "res1": res_other}

    def send_on(x, turn):
        return lax.ppermute(x, "owner", up if turn == 1 else down)

    units, kept, crossed, swapped = [], {}, {}, {}
    to_finish, to_place = [], []
    state = {"out": None, "token": None}

    def call(unit, rows, n_finish, n_place, after=()):
        finish = [to_finish.pop(0) for _ in range(max(0, n_finish))]
        place = [to_place.pop(0) for _ in range(max(0, n_place))]
        got = step_call(
            static,
            common,
            state["out"],
            None if unit is None else (unit, rows),
            [(units[f], kept[f], crossed[f]) for f in finish],
            [(units[p], swapped[p]) for p in place],
            [*after] if state["token"] is None else [state["token"], *after],
        )
        common.update({name: got[name] for name in ("meta", "spread", "res") if name in got})
        state["out"], state["token"] = got.get("out", state["out"]), got.get("token")
        if unit is not None:
            i = len(units)
            units.append(unit)
            kept[i] = got["kept"]
            crossed[i] = lax.ppermute(got["send"], "sector", swap_side)
            to_finish.append(i)
        for j, f in enumerate(finish):
            swapped[f] = lax.ppermute(got[f"swap{j}"], "sector", swap_core)
            to_place.append(f)

    last = n_owner - 1
    for step in range(last):
        unit = [(step, *lane) for lane in lanes]
        if state["token"] is not None:
            for i in range(len(xs) - 1, -1, -1):
                xs[i], state["token"] = lax.optimization_barrier((xs[i], state["token"]))
        if step < last - 1:
            then = [send_on(x, lane[0]) for x, lane in zip(xs, lanes, strict=True)]
        else:
            cut = [jnp.split(x, cuts, 2) for x in xs]
            then = [[send_on(x[0], lane[0]) for x, lane in zip(cut, lanes, strict=True)]]
        if step < last - 1:
            call(unit, xs, len(to_finish) - FINISH_LAG, len(to_place) - PLACE_LAG)
            xs = then
        else:
            call(unit, xs, 0, 0)
            for c in range(1, cuts):
                for x in cut:
                    x[c], state["token"] = lax.optimization_barrier((x[c], state["token"]))
                then.append([send_on(x[c], lane[0]) for x, lane in zip(cut, lanes, strict=True)])
            xs = then
    for c in range(cuts):
        unit = [(last, turn, start + c * (rows // cuts), rows // cuts) for turn, start, rows in lanes]
        if c < cuts - 1:
            call(unit, xs[c], len(to_finish) - 1, len(to_place))
        else:
            call(unit, xs[c], 0, 0, [crossed[i] for i in to_finish[:-1]])
    call(None, None, len(to_finish) - 1, len(to_place))
    call(None, None, 1, 0)
    call(None, None, 0, len(to_place) - 1)
    call(None, None, 0, 1)
    return state["out"][None, None]


def solution(mesh):
    in_specs = (
        P("sector", None, "owner", None),
        P("sector", "owner", None, None),
        P("sector", "owner", None, None),
        P("owner", None),
    )
    out_specs = P("sector", "owner", None, None, None)
    return jax.shard_map(shards, mesh=mesh, in_specs=in_specs, out_specs=out_specs, check_vma=False)
```
